32 devices in a mesh: plane: 16 (over z, y, core), depth: 2 (over x).
Axes of the slice: x: 2, y: 2, z: 4, core: 2. Of those that a mesh axis runs over, the one named last changes fastest.
Arguments:
- volume: float32 [64, 512, 256], P('plane', None, 'depth'), may hold values from -6 to 6
- resample: bfloat16 [512, 512], replicated, may hold values from 0 to 1, as said below
- transfer: float32 [16, 4], replicated, may hold values from 0.2 to 2
- light: float32 [3], replicated, may hold values from -4 to 4
- ray_bounds: int32 [2, 64, 512], replicated, may hold values from 0 to 256, as said below
Outputs:
- frame: float32 [4, 64, 512], P(None, 'plane', 'depth')
The draws below stay inside these ranges and needn't reach their ends.
Inputs may be any that keep to these rules, and one draw needn't show every extreme that they name: ray_bounds[0] < ray_bounds[1] for every pixel. `resample`: row v has nonzero entries only in columns v - 1, v and v + 1.
All inputs are finite; a program needn't handle non-finite values.
Results may differ from the reference program's by a relative error of at most 0.0003.
Values sent between devices are 32-bit elements; how exact they have to be, the bound alone decides.
A program may use at most 64 MiB of HBM per device.

```python
import math
import jax
import jax.numpy as jnp
from jax import lax

CX = 4
NY = 512
CZ = 128
KNOTS = 16
NX = 64
NZ = 256


def draw_resample(key, part):
    key_diag = jax.random.fold_in(key, 11)
    key_side = jax.random.fold_in(key, 12)
    diagonal = jax.random.uniform(key_diag, (NY,), jnp.float32, 0.55, 0.8)
    sides = jax.random.uniform(key_side, (2, NY), jnp.float32, 0.1, 0.25)
    rows = jnp.arange(NY, dtype=jnp.int32)[:, None]
    columns = jnp.arange(NY, dtype=jnp.int32)[None, :]
    matrix = diagonal[:, None] * (columns == rows).astype(jnp.float32)
    matrix = matrix + sides[0][:, None] * (columns == rows - 1).astype(jnp.float32)
    matrix = matrix + sides[1][:, None] * (columns == rows + 1).astype(jnp.float32)
    return matrix.astype(jnp.bfloat16)


def draw_ray_bounds(key, part):
    key_first = jax.random.fold_in(key, 21)
    key_last = jax.random.fold_in(key, 22)
    first = jax.random.randint(key_first, (NX, NY), 0, NZ // 2, dtype=jnp.int32)
    last = NZ - jax.random.randint(key_last, (NX, NY), 0, NZ // 2, dtype=jnp.int32)
    first = first.at[0, 0].set(0)
    last = last.at[0, 0].set(NZ)
    return jnp.stack([first, last]).astype(jnp.int32)


def levels(key, dims, shards, low, largest):
    loudness = 1.0
    for position, blocks in shards:
        heights = jax.random.uniform(jax.random.fold_in(jax.random.fold_in(key, 6), position), (blocks,), jnp.float32, low / len(shards), largest / len(shards))
        loudness = loudness * jnp.repeat(jnp.exp(heights), dims[position] // blocks).reshape((-1,) + (1,) * (len(dims) - 1 - position))
    return loudness


def gaussian(own_key, dims, scale, reach, split=(), kind=jnp.bfloat16):
    array = scale * jax.random.normal(own_key, dims, jnp.float32)
    if split:
        array = array * levels(own_key, dims, split, -0.22, 0.18)
    return jnp.clip(array, -reach, reach).astype(kind)


def setup_inputs(seed: int = 0) -> dict:
    streams_of = jax.random.split(jax.random.key(seed), 6)
    volume = gaussian(streams_of[0], (NX, NY, NZ), 1.0, 6.0, ((0, 16), (2, 2)), jnp.float32)
    resample = draw_resample(jax.random.fold_in(streams_of[5], 71), 0)
    transfer = jnp.clip(jnp.exp(jax.random.uniform(streams_of[2], (KNOTS, 4), jnp.float32, math.log(0.2), math.log(2.0))), 0.2, 2.0)
    light = gaussian(streams_of[3], (3,), 1.0, 4.0, (), jnp.float32)
    ray_bounds = draw_ray_bounds(jax.random.fold_in(streams_of[5], 71), 0)
    return dict(volume=volume, resample=resample, transfer=transfer, light=light, ray_bounds=ray_bounds)


def central(field, axis):
    widths = [(1, 1) if dim == axis else (0, 0) for dim in range(3)]
    padded = jnp.pad(field, widths)
    size = field.shape[axis]
    upper = lax.slice_in_dim(padded, 2, size + 2, axis=axis)
    lower = lax.slice_in_dim(padded, 0, size, axis=axis)
    return (upper - lower) * 0.5

def shade(density, grad_x, grad_y, grad_z, transfer, light):
    scaled = jnp.clip((density + 2.5) / 5.0, 0.0, 1.0) * (transfer.shape[0] - 1)
    sigma = jnp.zeros_like(density)
    red = jnp.zeros_like(density)
    green = jnp.zeros_like(density)
    blue = jnp.zeros_like(density)
    for knot in range(transfer.shape[0]):
        hat = jnp.maximum(0.0, 1.0 - jnp.abs(scaled - knot))
        sigma = sigma + hat * transfer[knot, 3]
        red = red + hat * transfer[knot, 0]
        green = green + hat * transfer[knot, 1]
        blue = blue + hat * transfer[knot, 2]
    lit = jnp.abs(grad_x * light[0] + grad_y * light[1] + grad_z * light[2])
    lit = 0.3 + 0.7 * lit / jnp.sqrt(grad_x * grad_x + grad_y * grad_y + grad_z * grad_z + 1.0)
    return (sigma, red * lit, green * lit, blue * lit)

def reference(volume, resample, transfer, light, ray_bounds):
    fields = jnp.stack([volume.astype(jnp.bfloat16), central(volume, 0).astype(jnp.bfloat16), central(volume, 1).astype(jnp.bfloat16), central(volume, 2).astype(jnp.bfloat16)])
    group = CZ // CX
    row_block = NY // 8
    step_size = 2.0 / NZ

    def render(row_start):
        weights = lax.dynamic_slice_in_dim(resample, row_start, row_block, 0)
        samples = lax.dot_general(weights, fields, (((1,), (2,)), ((), ())), preferred_element_type=jnp.float32)
        sigma, red, green, blue = shade(samples[:, 0], samples[:, 1], samples[:, 2], samples[:, 3], transfer, light)
        channels = jnp.stack([sigma, red, green, blue])
        pieces = []
        for offset in range(NZ // group):
            piece = channels[:, :, :, offset * group:(offset + 1) * group]
            piece = jnp.pad(piece, ((0, 0), (0, 0), (offset, 0), (0, 0)))[:, :, :NX]
            pieces.append(piece)
        sheared = jnp.concatenate(pieces, axis=3)
        first = lax.dynamic_slice_in_dim(ray_bounds[0], row_start, row_block, 1).T
        last = lax.dynamic_slice_in_dim(ray_bounds[1], row_start, row_block, 1).T
        sample_index = jnp.arange(NZ, dtype=jnp.int32)
        inside = (sample_index >= first[:, :, None]) & (sample_index < last[:, :, None])
        tau = step_size * sheared[0] * inside.astype(jnp.float32)
        before = jnp.cumsum(tau, axis=2) - tau
        weight = jnp.exp(-before) * (1.0 - jnp.exp(-tau))
        color = lax.optimization_barrier(jnp.sum(weight[None] * sheared[1:], axis=3))
        opacity = 1.0 - jnp.exp(-lax.optimization_barrier(jnp.sum(tau, axis=2)))
        return jnp.concatenate([color, opacity[None]], axis=0)
    starts = jnp.arange(0, NY, row_block, dtype=jnp.int32)
    blocks = lax.map(render, starts)
    return blocks.transpose(1, 3, 0, 2).reshape(4, NX, NY)
```

```python
import functools

import jax
import jax.numpy as jnp
from jax import lax
from jax.experimental import pallas as pl
from jax.experimental.pallas import tpu as pltpu
from jax.sharding import PartitionSpec as P

MESH = pl.DeviceIdType.MESH
PAD = 8


def kernel(
    planes, depths, volume, resample, bounds, transfer, light, out,
    vol, mat, rows, window, side_x, edge, side_z, tall, fields, samples, taus, before, tint, pieces,
    table, send, recv, local_sem, x_send, x_recv, z_send, z_recv, p_send, p_recv,
):
    cells_x, cells_y, cells_z = volume.shape
    knots = transfer.shape[0]
    columns = bounds.shape[1]
    share = cells_y // depths
    group = cells_z // cells_x
    lanes = 128
    p = lax.axis_index("plane")
    d = lax.axis_index("depth")

    loads = [pltpu.make_async_copy(volume.at[x], vol.at[x], local_sem.at[x]) for x in range(cells_x)]
    loads.append(pltpu.make_async_copy(resample, mat, local_sem.at[cells_x]))
    loads.append(pltpu.make_async_copy(bounds, rows.at[:, :columns], local_sem.at[cells_x + 1]))
    for load in loads:
        load.start()

    barrier = pltpu.get_barrier_semaphore()

    def greet(condition, plane, depth):
        @pl.when(condition)
        def _():
            pl.semaphore_signal(barrier, inc=1, device_id=(plane, depth), device_id_type=MESH)

    greet(p > 0, p - 1, d)
    greet(p < planes - 1, p + 1, d)
    greet(d > 0, p, d - 1)
    greet(d < depths - 1, p, d + 1)
    for source in range(depths):
        low_there = p - source >= 0
        if source == 0:
            low_there = low_there & (d != 0)
        greet(low_there, p - source, source)
        greet(p - source - 1 >= 0, p - source - 1, source)

    table[...] = jnp.zeros_like(table)
    table[:knots, : transfer.shape[1]] = transfer[...]
    flat = table[...].T[:8]
    knot_index = lax.broadcasted_iota(jnp.int32, flat.shape, 1)
    slope = jnp.where(knot_index < knots - 1, pltpu.roll(flat, lanes - 1, 1) - flat, 0.0)
    table[:8] = flat
    table[8:16] = slope

    for x in range(cells_x):
        loads[x].wait()

    def turn(x, carry):
        turned = vol[x].T
        tall[x + 1, PAD : PAD + cells_z] = turned
        fields[0, x] = turned.astype(jnp.bfloat16)
        edge[0, x] = turned[:1]
        edge[1, x] = turned[cells_z - 1 :]
        return carry

    lax.fori_loop(0, cells_x, turn, 0)

    def one(condition):
        return jnp.where(condition, 1, 0)

    partners = one(p > 0) + one(p < planes - 1) + one(d > 0) + one(d < depths - 1)
    partners += one(p + d < planes) * (depths - one(d == 0))
    partners += one(p + d + 1 < planes) * depths
    pl.semaphore_wait(barrier, partners)

    def remote(src, dst, send_sem, recv_sem, plane, depth):
        return pltpu.make_async_remote_copy(
            src_ref=src, dst_ref=dst, send_sem=send_sem, recv_sem=recv_sem,
            device_id=(plane, depth), device_id_type=MESH,
        )

    x_up = remote(vol.at[cells_x - 1], side_x.at[0], x_send.at[0], x_recv.at[0], p + 1, d)
    x_down = remote(vol.at[0], side_x.at[1], x_send.at[1], x_recv.at[1], p - 1, d)
    z_up = remote(edge.at[1], side_z.at[0], z_send.at[0], z_recv.at[0], p, d + 1)
    z_down = remote(edge.at[0], side_z.at[1], z_send.at[1], z_recv.at[1], p, d - 1)
    has_below, has_above = p > 0, p < planes - 1
    has_front, has_back = d > 0, d < depths - 1
    pl.when(has_above)(x_up.start)
    pl.when(has_below)(x_down.start)
    pl.when(has_back)(z_up.start)
    pl.when(has_front)(z_down.start)

    def resampled(field, first, count):
        for x in range(first, first + count):
            samples[field, x] = lax.dot_general(
                fields[field, x], mat[...], (((1,), (1,)), ((), ())),
                preferred_element_type=jnp.float32,
            )

    loads[cells_x].wait()
    resampled(0, 0, cells_x)

    def slope_y(step, carry):
        x, part = step // cells_x, step % cells_x
        block = tall[x + 1, pl.ds(pl.multiple_of(PAD + part * group, 8), group)]
        lane = lax.broadcasted_iota(jnp.int32, block.shape, 1)
        upper = jnp.where(lane < cells_y - 1, pltpu.roll(block, cells_y - 1, 1), 0.0)
        lower = jnp.where(lane > 0, pltpu.roll(block, 1, 1), 0.0)
        fields[2, x, pl.ds(pl.multiple_of(part * group, 16), group)] = (
            (upper - lower) * 0.5
        ).astype(jnp.bfloat16)
        return carry

    lax.fori_loop(0, cells_x * cells_x, slope_y, 0)
    resampled(2, 0, cells_x)

    loads[cells_x + 1].wait()
    rows[:, columns:] = jnp.zeros_like(rows[:, columns:])
    nearest = jnp.minimum(p + d, planes - 1) * cells_x
    offset = nearest % 8
    around = pl.ds(pl.multiple_of(nearest - offset, 8), 16)
    for end in range(2):
        found = rows[end, around]
        aligned = jnp.where(offset == 0, found[: 2 * cells_x], found[8 - cells_x : 8 + cells_x])
        for pixel in range(2 * cells_x):
            window[end, pixel] = aligned[pixel : pixel + 1]

    scale = (knots - 1) / 5.0
    step_size = 2.0 / (depths * cells_z)

    def density(step, carry):
        x, part = step // cells_x, step % cells_x
        at = pl.ds(pl.multiple_of(part * group, 16), group)
        index = d * cells_z + part * group + lax.broadcasted_iota(jnp.int32, (group, lanes), 0)
        for tile in range(cells_y // lanes):
            here = slice(tile * lanes, (tile + 1) * lanes)
            spot = jnp.clip(samples[0, x, at, here] * scale + 2.5 * scale, 0.0, knots - 1.0)
            knot = spot.astype(jnp.int32)
            rest = spot - knot.astype(jnp.float32)

            def looked_up(channel):
                base = jnp.broadcast_to(table[channel : channel + 1], (group, lanes))
                tilt = jnp.broadcast_to(table[8 + channel : 9 + channel], (group, lanes))
                return jnp.take_along_axis(
                    base, knot, axis=1, mode="promise_in_bounds"
                ) + rest * jnp.take_along_axis(tilt, knot, axis=1, mode="promise_in_bounds")

            first = window[0, x + part, :, here]
            last = window[1, x + part, :, here]
            inside = (index >= first) & (index < last)
            taus[x, at, here] = jnp.where(inside, step_size * looked_up(3), 0.0)
            for channel in range(3):
                tint[channel, x, at, here] = looked_up(channel)
        return carry

    lax.fori_loop(0, cells_x * cells_x, density, 0)

    row = lax.broadcasted_iota(jnp.int32, (cells_z, cells_z), 0)
    column = lax.broadcasted_iota(jnp.int32, (cells_z, cells_z), 1)
    earlier = jnp.where((column < row) & (column // group == row // group), 1.0, 0.0)
    earlier = earlier.astype(jnp.bfloat16)
    for x in range(cells_x):
        tau = taus[x]
        high = tau.astype(jnp.bfloat16)
        low = (tau - high.astype(jnp.float32)).astype(jnp.bfloat16)
        before[x] = jnp.dot(earlier, high, preferred_element_type=jnp.float32) + jnp.dot(
            earlier, low, preferred_element_type=jnp.float32
        )

    pl.when(has_front)(z_down.wait_send)
    pl.when(has_back)(z_up.wait_send)
    pl.when(has_front)(z_up.wait_recv)
    pl.when(has_back)(z_down.wait_recv)

    @pl.when(jnp.logical_not(has_front))
    def _():
        side_z[0] = jnp.zeros_like(side_z[0])

    @pl.when(jnp.logical_not(has_back))
    def _():
        side_z[1] = jnp.zeros_like(side_z[1])

    for x in range(cells_x):
        tall[x + 1, PAD - 1 : PAD] = side_z[0, x]
        tall[x + 1, PAD + cells_z : PAD + cells_z + 1] = side_z[1, x]
    for x in range(cells_x):
        ahead = tall[x + 1, PAD + 1 : PAD + 1 + cells_z]
        behind = tall[x + 1, PAD - 1 : PAD - 1 + cells_z]
        fields[3, x] = ((ahead - behind) * 0.5).astype(jnp.bfloat16)
    resampled(3, 0, cells_x)

    def slope_x(x, carry):
        ahead = tall[x + 2, PAD : PAD + cells_z]
        behind = tall[x, PAD : PAD + cells_z]
        fields[1, x] = ((ahead - behind) * 0.5).astype(jnp.bfloat16)
        return carry

    lax.fori_loop(1, cells_x - 1, slope_x, 0)
    resampled(1, 1, cells_x - 2)
    pl.when(has_above)(x_up.wait_send)
    pl.when(has_below)(x_down.wait_send)
    pl.when(has_below)(x_up.wait_recv)
    pl.when(has_above)(x_down.wait_recv)

    @pl.when(jnp.logical_not(has_below))
    def _():
        side_x[0] = jnp.zeros_like(side_x[0])

    @pl.when(jnp.logical_not(has_above))
    def _():
        side_x[1] = jnp.zeros_like(side_x[1])

    tall[0, PAD : PAD + cells_z] = side_x[0].T
    tall[cells_x + 1, PAD : PAD + cells_z] = side_x[1].T
    slope_x(0, 0)
    slope_x(cells_x - 1, 0)
    resampled(1, 0, 1)
    resampled(1, cells_x - 1, 1)

    light_x, light_y, light_z = light[0], light[1], light[2]

    def composite(step, carry):
        x, part = step // cells_x, step % cells_x
        at = pl.ds(pl.multiple_of(part * group, 16), group)
        for tile in range(cells_y // lanes):
            here = slice(tile * lanes, (tile + 1) * lanes)
            grad_x = samples[1, x, at, here]
            grad_y = samples[2, x, at, here]
            grad_z = samples[3, x, at, here]
            lit = jnp.abs(grad_x * light_x + grad_y * light_y + grad_z * light_z)
            norm = grad_x * grad_x + grad_y * grad_y + grad_z * grad_z + 1.0
            lit = 0.3 + 0.7 * lit * lax.rsqrt(norm)
            tau = taus[x, at, here]
            weight = jnp.exp(-before[x, at, here]) * (1.0 - jnp.exp(-tau)) * lit
            for channel in range(3):
                pieces[part, channel, x, :, here] = jnp.sum(
                    weight * tint[channel, x, at, here], axis=0, keepdims=True
                )
            pieces[part, 3, x, :, here] = jnp.sum(tau, axis=0, keepdims=True)
        return carry

    lax.fori_loop(0, cells_x * cells_x, composite, 0)

    def placed(part, channel):
        ahead = [jnp.zeros((part, cells_y), jnp.float32)] if part else []
        block = [pieces[part, channel, x] for x in range(cells_x)]
        rest = [jnp.zeros((cells_x - part, cells_y), jnp.float32)]
        return jnp.concatenate(ahead + block + rest, axis=0)

    color, remain = None, None
    for part in range(cells_x - 1, -1, -1):
        clear = jnp.exp(-placed(part, 3))
        front = [placed(part, channel) for channel in range(3)]
        if color is None:
            color, remain = front, clear
        else:
            color = [front[channel] + clear * color[channel] for channel in range(3)]
            remain = clear * remain
    for channel, value in enumerate(color + [remain]):
        for half in range(2):
            for block in range(depths):
                send[half, block, channel] = value[
                    half * cells_x : (half + 1) * cells_x, block * share : (block + 1) * share
                ]

    sends = []
    for half in range(2):
        for block in range(depths):
            there = p + d + half < planes
            if half == 0 and block == 0:
                there = there & (d != 0)
            copy = remote(
                send.at[half, block], recv.at[d, half], p_send.at[half, block],
                p_recv.at[d, half], p + d + half, block,
            )
            pl.when(there)(copy.start)
            sends.append((there, copy))

    @pl.when(d == 0)
    def _():
        recv[0, 0] = send[0, 0]

    for source in range(depths):
        for half in range(2):
            there = p - source - half >= 0

            @pl.when(jnp.logical_not(there))
            def _():
                recv[source, half, :3] = jnp.zeros_like(recv[source, half, :3])
                recv[source, half, 3] = jnp.ones_like(recv[source, half, 3])

            if half == 0 and source == 0:
                there = there & (d != 0)
            arrival = remote(
                send.at[half, 0], recv.at[source, half], p_send.at[half, 0],
                p_recv.at[source, half], p, d,
            )
            pl.when(there)(arrival.wait_recv)

    color = [recv[0, 0, channel] for channel in range(3)]
    remain = recv[0, 0, 3]
    for source in range(depths):
        for half in range(2):
            if source == 0 and half == 0:
                continue
            color = [
                color[channel] + remain * recv[source, half, channel] for channel in range(3)
            ]
            remain = remain * recv[source, half, 3]
    for channel in range(3):
        out[channel] = color[channel]
    out[3] = 1.0 - remain
    for there, copy in sends:
        pl.when(there)(copy.wait_send)


def body(volume, resample, transfer, light, ray_bounds):
    cells_x, cells_y, cells_z = volume.shape
    planes = lax.axis_size("plane")
    depths = lax.axis_size("depth")
    share = cells_y // depths
    f32 = jnp.float32
    dma = pltpu.SemaphoreType.DMA
    return pl.pallas_call(
        functools.partial(kernel, planes, depths),
        out_shape=jax.ShapeDtypeStruct((4, cells_x, share), f32),
        in_specs=[
            pl.BlockSpec(memory_space=pl.ANY),
            pl.BlockSpec(memory_space=pl.ANY),
            pl.BlockSpec(memory_space=pl.ANY),
            pl.BlockSpec(memory_space=pltpu.VMEM),
            pl.BlockSpec(memory_space=pltpu.SMEM),
        ],
        out_specs=pl.BlockSpec(memory_space=pltpu.VMEM),
        scratch_shapes=[
            pltpu.VMEM((cells_x, cells_y, cells_z), f32),
            pltpu.VMEM(resample.shape, resample.dtype),
            pltpu.VMEM((2, ray_bounds.shape[1] + 8, cells_y), ray_bounds.dtype),
            pltpu.VMEM((2, 2 * cells_x, 1, cells_y), ray_bounds.dtype),
            pltpu.VMEM((2, cells_y, cells_z), f32),
            pltpu.VMEM((2, cells_x, 1, cells_y), f32),
            pltpu.VMEM((2, cells_x, 1, cells_y), f32),
            pltpu.VMEM((cells_x + 2, cells_z + 2 * PAD, cells_y), f32),
            pltpu.VMEM((4, cells_x, cells_z, cells_y), jnp.bfloat16),
            pltpu.VMEM((4, cells_x, cells_z, cells_y), f32),
            pltpu.VMEM((cells_x, cells_z, cells_y), f32),
            pltpu.VMEM((cells_x, cells_z, cells_y), f32),
            pltpu.VMEM((3, cells_x, cells_z, cells_y), f32),
            pltpu.VMEM((cells_x, 4, cells_x, 1, cells_y), f32),
            pltpu.VMEM((128, 128), f32),
            pltpu.VMEM((2, depths, 4, cells_x, share), f32),
            pltpu.VMEM((depths, 2, 4, cells_x, share), f32),
            dma((cells_x + 2,)),
            dma((2,)),
            dma((2,)),
            dma((2,)),
            dma((2,)),
            dma((2, depths)),
            dma((depths, 2)),
        ],
        compiler_params=pltpu.CompilerParams(
            collective_id=0, has_side_effects=True, vmem_limit_bytes=40 * 1024 * 1024
        ),
    )(volume, resample, ray_bounds, transfer, light)


def solution(mesh):
    in_specs = (P("plane", None, "depth"), P(), P(), P(), P())
    out_specs = P(None, "plane", "depth")
    return jax.shard_map(body, mesh=mesh, in_specs=in_specs, out_specs=out_specs, check_vma=False)
```

```python
import functools

import jax
import jax.numpy as jnp
from jax import lax
from jax.experimental import pallas as pl
from jax.experimental.pallas import tpu as pltpu
from jax.sharding import PartitionSpec as P

MESH = pl.DeviceIdType.MESH
PAD = 8


def kernel(
    planes, depths, volume, resample, bounds, transfer, light, out,
    vol, mat, rows, window, side_x, edge, side_z, tall, fields, samples, taus, before, tint, pieces,
    table, send, recv, local_sem, x_send, x_recv, z_send, z_recv, p_send, p_recv,
):
    cells_x, cells_y, cells_z = volume.shape
    channels, knots = transfer.shape
    columns = bounds.shape[1]
    share = cells_y // depths
    group = cells_z // cells_x
    lanes = 128
    p = lax.axis_index("plane")
    d = lax.axis_index("depth")

    loads = [pltpu.make_async_copy(volume.at[x], vol.at[x], local_sem.at[x]) for x in range(cells_x)]
    loads.append(pltpu.make_async_copy(resample, mat, local_sem.at[cells_x]))
    loads.append(pltpu.make_async_copy(bounds, rows.at[:, :columns], local_sem.at[cells_x + 1]))
    for load in loads:
        load.start()

    barrier = pltpu.get_barrier_semaphore()

    def greet(condition, plane, depth):
        @pl.when(condition)
        def _():
            pl.semaphore_signal(barrier, inc=1, device_id=(plane, depth), device_id_type=MESH)

    greet(p > 0, p - 1, d)
    greet(p < planes - 1, p + 1, d)
    greet(d > 0, p, d - 1)
    greet(d < depths - 1, p, d + 1)
    for source in range(depths):
        low_there = p - source >= 0
        if source == 0:
            low_there = low_there & (d != 0)
        greet(low_there, p - source, source)
        greet(p - source - 1 >= 0, p - source - 1, source)

    table[...] = jnp.zeros_like(table)
    table[:channels, :knots] = transfer[...]
    flat = table[:8]
    knot_index = lax.broadcasted_iota(jnp.int32, flat.shape, 1)
    slope = jnp.where(knot_index < knots - 1, pltpu.roll(flat, lanes - 1, 1) - flat, 0.0)
    table[8:16] = slope

    def one(condition):
        return jnp.where(condition, 1, 0)

    partners = one(p > 0) + one(p < planes - 1) + one(d > 0) + one(d < depths - 1)
    partners += one(p + d < planes) * (depths - one(d == 0))
    partners += one(p + d + 1 < planes) * depths
    pl.semaphore_wait(barrier, partners)

    def remote(src, dst, send_sem, recv_sem, plane, depth):
        return pltpu.make_async_remote_copy(
            src_ref=src, dst_ref=dst, send_sem=send_sem, recv_sem=recv_sem,
            device_id=(plane, depth), device_id_type=MESH,
        )

    x_up = remote(volume.at[cells_x - 1], side_x.at[0], x_send.at[0], x_recv.at[0], p + 1, d)
    x_down = remote(volume.at[0], side_x.at[1], x_send.at[1], x_recv.at[1], p - 1, d)
    z_up = remote(edge.at[1], side_z.at[0], z_send.at[0], z_recv.at[0], p, d + 1)
    z_down = remote(edge.at[0], side_z.at[1], z_send.at[1], z_recv.at[1], p, d - 1)
    has_below, has_above = p > 0, p < planes - 1
    has_front, has_back = d > 0, d < depths - 1
    pl.when(has_above)(x_up.start)
    pl.when(has_below)(x_down.start)
    for x in range(cells_x):
        loads[x].wait()

    def turn(x, carry):
        turned = vol[x].T
        tall[x + 1, PAD : PAD + cells_z] = turned
        fields[0, x] = turned.astype(jnp.bfloat16)
        edge[0, x] = turned[:1]
        edge[1, x] = turned[cells_z - 1 :]
        return carry

    lax.fori_loop(0, cells_x, turn, 0, unroll=True)

    pl.when(has_back)(z_up.start)
    pl.when(has_front)(z_down.start)

    def resampled(field, first, count):
        block = fields[field, first : first + count].reshape(count * cells_z, cells_y)
        found = lax.dot_general(
            block, mat[...], (((1,), (1,)), ((), ())), preferred_element_type=jnp.float32
        )
        samples[field, first : first + count] = found.reshape(count, cells_z, cells_y)

    loads[cells_x].wait()
    resampled(0, 0, cells_x)

    def slope_y(step, carry):
        x, part = step // cells_x, step % cells_x
        block = tall[x + 1, pl.ds(pl.multiple_of(PAD + part * group, 8), group)]
        lane = lax.broadcasted_iota(jnp.int32, block.shape, 1)
        upper = jnp.where(lane < cells_y - 1, pltpu.roll(block, cells_y - 1, 1), 0.0)
        lower = jnp.where(lane > 0, pltpu.roll(block, 1, 1), 0.0)
        fields[2, x, pl.ds(pl.multiple_of(part * group, 16), group)] = (
            (upper - lower) * 0.5
        ).astype(jnp.bfloat16)
        return carry

    lax.fori_loop(0, cells_x * cells_x, slope_y, 0, unroll=True)
    resampled(2, 0, cells_x)

    loads[cells_x + 1].wait()
    rows[:, columns:] = jnp.zeros_like(rows[:, columns:])
    nearest = jnp.minimum(p + d, planes - 1) * cells_x
    offset = nearest % 8
    around = pl.ds(pl.multiple_of(nearest - offset, 8), 16)
    for end in range(2):
        found = rows[end, around]
        aligned = jnp.where(offset == 0, found[: 2 * cells_x], found[8 - cells_x : 8 + cells_x])
        for pixel in range(2 * cells_x):
            window[end, pixel] = aligned[pixel : pixel + 1]

    scale = (knots - 1) / 5.0
    step_size = 2.0 / (depths * cells_z)

    def density(step, carry):
        x, part = step // cells_x, step % cells_x
        at = pl.ds(pl.multiple_of(part * group, 16), group)
        index = d * cells_z + part * group + lax.broadcasted_iota(jnp.int32, (group, lanes), 0)
        for tile in range(cells_y // lanes):
            here = slice(tile * lanes, (tile + 1) * lanes)
            spot = jnp.clip(samples[0, x, at, here] * scale + 2.5 * scale, 0.0, knots - 1.0)
            knot = spot.astype(jnp.int32)
            rest = spot - knot.astype(jnp.float32)

            def looked_up(channel):
                base = jnp.broadcast_to(table[channel : channel + 1], (group, lanes))
                tilt = jnp.broadcast_to(table[8 + channel : 9 + channel], (group, lanes))
                return jnp.take_along_axis(
                    base, knot, axis=1, mode="promise_in_bounds"
                ) + rest * jnp.take_along_axis(tilt, knot, axis=1, mode="promise_in_bounds")

            first = window[0, x + part, :, here]
            last = window[1, x + part, :, here]
            inside = (index >= first) & (index < last)
            taus[x, at, here] = jnp.where(inside, step_size * looked_up(3), 0.0)
            for channel in range(3):
                tint[channel, x, at, here] = looked_up(channel)
        return carry

    lax.fori_loop(0, cells_x * cells_x, density, 0, unroll=True)

    row = lax.broadcasted_iota(jnp.int32, (cells_z, cells_z), 0)
    column = lax.broadcasted_iota(jnp.int32, (cells_z, cells_z), 1)
    earlier = jnp.where((column < row) & (column // group == row // group), 1.0, 0.0)
    earlier = earlier.astype(jnp.bfloat16)
    earlier = jnp.concatenate([earlier, earlier], axis=1)
    for x in range(cells_x):
        tau = taus[x]
        high = tau.astype(jnp.bfloat16)
        low = (tau - high.astype(jnp.float32)).astype(jnp.bfloat16)
        before[x] = jnp.dot(
            earlier, jnp.concatenate([high, low], axis=0), preferred_element_type=jnp.float32
        )

    pl.when(has_front)(z_down.wait_send)
    pl.when(has_back)(z_up.wait_send)
    pl.when(has_front)(z_up.wait_recv)
    pl.when(has_back)(z_down.wait_recv)

    @pl.when(jnp.logical_not(has_front))
    def _():
        side_z[0] = jnp.zeros_like(side_z[0])

    @pl.when(jnp.logical_not(has_back))
    def _():
        side_z[1] = jnp.zeros_like(side_z[1])

    for x in range(cells_x):
        tall[x + 1, PAD - 1 : PAD] = side_z[0, x]
        tall[x + 1, PAD + cells_z : PAD + cells_z + 1] = side_z[1, x]
    for x in range(cells_x):
        ahead = tall[x + 1, PAD + 1 : PAD + 1 + cells_z]
        behind = tall[x + 1, PAD - 1 : PAD - 1 + cells_z]
        fields[3, x] = ((ahead - behind) * 0.5).astype(jnp.bfloat16)
    resampled(3, 0, cells_x)

    light_x, light_y, light_z = light[0], light[1], light[2]

    def composite(first, step, carry):
        x, part = first + step // cells_x, step % cells_x
        at = pl.ds(pl.multiple_of(part * group, 16), group)
        for tile in range(cells_y // lanes):
            here = slice(tile * lanes, (tile + 1) * lanes)
            grad_x = samples[1, (x - 1) % cells_x, at, here]
            grad_y = samples[2, x, at, here]
            grad_z = samples[3, x, at, here]
            lit = jnp.abs(grad_x * light_x + grad_y * light_y + grad_z * light_z)
            norm = grad_x * grad_x + grad_y * grad_y + grad_z * grad_z + 1.0
            lit = 0.3 + 0.7 * lit * lax.rsqrt(norm)
            tau = taus[x, at, here]
            weight = jnp.exp(-before[x, at, here]) * (1.0 - jnp.exp(-tau)) * lit
            for channel in range(3):
                pieces[part, channel, x, :, here] = jnp.sum(
                    weight * tint[channel, x, at, here], axis=0, keepdims=True
                )
            pieces[part, 3, x, :, here] = jnp.sum(tau, axis=0, keepdims=True)
        return carry

    def composited(first, count):
        lax.fori_loop(
            0, count * cells_x, functools.partial(composite, first), 0, unroll=True
        )

    def slope_x(x):
        ahead = tall[x + 2, PAD : PAD + cells_z]
        behind = tall[x, PAD : PAD + cells_z]
        fields[1, (x - 1) % cells_x] = ((ahead - behind) * 0.5).astype(jnp.bfloat16)

    for x in range(1, cells_x - 1):
        slope_x(x)
    resampled(1, 0, cells_x - 2)
    composited(1, cells_x - 2)
    pl.when(has_above)(x_up.wait_send)
    pl.when(has_below)(x_down.wait_send)
    pl.when(has_below)(x_up.wait_recv)
    pl.when(has_above)(x_down.wait_recv)

    @pl.when(jnp.logical_not(has_below))
    def _():
        side_x[0] = jnp.zeros_like(side_x[0])

    @pl.when(jnp.logical_not(has_above))
    def _():
        side_x[1] = jnp.zeros_like(side_x[1])

    tall[0, PAD : PAD + cells_z] = side_x[0].T
    tall[cells_x + 1, PAD : PAD + cells_z] = side_x[1].T
    slope_x(0)
    slope_x(cells_x - 1)
    resampled(1, cells_x - 2, 2)
    composited(0, 1)
    composited(cells_x - 1, 1)

    def placed(part, channel):
        ahead = [jnp.zeros((part, cells_y), jnp.float32)] if part else []
        block = [pieces[part, channel, x] for x in range(cells_x)]
        rest = [jnp.zeros((cells_x - part, cells_y), jnp.float32)]
        return jnp.concatenate(ahead + block + rest, axis=0)

    color, remain = None, None
    for part in range(cells_x - 1, -1, -1):
        clear = jnp.exp(-placed(part, 3))
        front = [placed(part, channel) for channel in range(3)]
        if color is None:
            color, remain = front, clear
        else:
            color = [front[channel] + clear * color[channel] for channel in range(3)]
            remain = clear * remain
    for channel, value in enumerate(color + [remain]):
        for half in range(2):
            for block in range(depths):
                send[half, block, channel] = value[
                    half * cells_x : (half + 1) * cells_x, block * share : (block + 1) * share
                ]

    sends = []
    for half in range(2):
        for block in range(depths):
            there = p + d + half < planes
            if half == 0 and block == 0:
                there = there & (d != 0)
            copy = remote(
                send.at[half, block], recv.at[d, half], p_send.at[half, block],
                p_recv.at[d, half], p + d + half, block,
            )
            pl.when(there)(copy.start)
            sends.append((there, copy))

    @pl.when(d == 0)
    def _():
        recv[0, 0] = send[0, 0]

    for source in range(depths):
        for half in range(2):
            there = p - source - half >= 0

            @pl.when(jnp.logical_not(there))
            def _():
                recv[source, half, :3] = jnp.zeros_like(recv[source, half, :3])
                recv[source, half, 3] = jnp.ones_like(recv[source, half, 3])

            if half == 0 and source == 0:
                there = there & (d != 0)
            arrival = remote(
                send.at[half, 0], recv.at[source, half], p_send.at[half, 0],
                p_recv.at[source, half], p, d,
            )
            pl.when(there)(arrival.wait_recv)

    color = [recv[0, 0, channel] for channel in range(3)]
    remain = recv[0, 0, 3]
    for source in range(depths):
        for half in range(2):
            if source == 0 and half == 0:
                continue
            color = [
                color[channel] + remain * recv[source, half, channel] for channel in range(3)
            ]
            remain = remain * recv[source, half, 3]
    for channel in range(3):
        out[channel] = color[channel]
    out[3] = 1.0 - remain
    for there, copy in sends:
        pl.when(there)(copy.wait_send)


def body(volume, resample, transfer, light, ray_bounds):
    cells_x, cells_y, cells_z = volume.shape
    planes = lax.axis_size("plane")
    depths = lax.axis_size("depth")
    share = cells_y // depths
    f32 = jnp.float32
    dma = pltpu.SemaphoreType.DMA
    return pl.pallas_call(
        functools.partial(kernel, planes, depths),
        out_shape=jax.ShapeDtypeStruct((4, cells_x, share), f32),
        in_specs=[
            pl.BlockSpec(memory_space=pltpu.HBM),
            pl.BlockSpec(memory_space=pltpu.HBM),
            pl.BlockSpec(memory_space=pltpu.HBM),
            pl.BlockSpec(memory_space=pltpu.VMEM),
            pl.BlockSpec(memory_space=pltpu.SMEM),
        ],
        out_specs=pl.BlockSpec(memory_space=pltpu.VMEM),
        scratch_shapes=[
            pltpu.VMEM((cells_x, cells_y, cells_z), f32),
            pltpu.VMEM(resample.shape, resample.dtype),
            pltpu.VMEM((2, ray_bounds.shape[1] + 8, cells_y), ray_bounds.dtype),
            pltpu.VMEM((2, 2 * cells_x, 1, cells_y), ray_bounds.dtype),
            pltpu.VMEM((2, cells_y, cells_z), f32),
            pltpu.VMEM((2, cells_x, 1, cells_y), f32),
            pltpu.VMEM((2, cells_x, 1, cells_y), f32),
            pltpu.VMEM((cells_x + 2, cells_z + 2 * PAD, cells_y), f32),
            pltpu.VMEM((4, cells_x, cells_z, cells_y), jnp.bfloat16),
            pltpu.VMEM((4, cells_x, cells_z, cells_y), f32),
            pltpu.VMEM((cells_x, cells_z, cells_y), f32),
            pltpu.VMEM((cells_x, cells_z, cells_y), f32),
            pltpu.VMEM((3, cells_x, cells_z, cells_y), f32),
            pltpu.VMEM((cells_x, 4, cells_x, 1, cells_y), f32),
            pltpu.VMEM((16, 128), f32),
            pltpu.VMEM((2, depths, 4, cells_x, share), f32),
            pltpu.VMEM((depths, 2, 4, cells_x, share), f32),
            dma((cells_x + 2,)),
            dma((2,)),
            dma((2,)),
            dma((2,)),
            dma((2,)),
            dma((2, depths)),
            dma((depths, 2)),
        ],
        compiler_params=pltpu.CompilerParams(
            collective_id=0, has_side_effects=True, vmem_limit_bytes=40 * 1024 * 1024
        ),
    )(volume, resample, ray_bounds, transfer.T, light)


def solution(mesh):
    in_specs = (P("plane", None, "depth"), P(), P(), P(), P())
    out_specs = P(None, "plane", "depth")
    return jax.shard_map(body, mesh=mesh, in_specs=in_specs, out_specs=out_specs, check_vma=False)
```

```python
import functools

import jax
import jax.numpy as jnp
from jax import lax
from jax.experimental import pallas as pl
from jax.experimental.pallas import tpu as pltpu
from jax.sharding import PartitionSpec as P

MESH = pl.DeviceIdType.MESH
PAD = 8


def kernel(
    planes, depths, volume, resample, bounds, transfer, light, out,
    vol, mat, rows, window, side_x, edge, side_z, tall, fields, samples, taus, before, tint, pieces,
    table, send, recv, local_sem, x_send, x_recv, z_send, z_recv, p_send, p_recv,
):
    cells_x, cells_y, cells_z = volume.shape
    channels, knots = transfer.shape
    columns = bounds.shape[1]
    share = cells_y // depths
    group = cells_z // cells_x
    lanes = 128
    p = lax.axis_index("plane")
    d = lax.axis_index("depth")

    loads = [pltpu.make_async_copy(volume.at[x], vol.at[x], local_sem.at[x]) for x in range(cells_x)]
    loads.append(pltpu.make_async_copy(resample, mat, local_sem.at[cells_x]))
    loads.append(pltpu.make_async_copy(bounds, rows.at[:, :columns], local_sem.at[cells_x + 1]))
    for load in loads:
        load.start()

    barrier = pltpu.get_barrier_semaphore()

    def greet(condition, plane, depth):
        @pl.when(condition)
        def _():
            pl.semaphore_signal(barrier, inc=1, device_id=(plane, depth), device_id_type=MESH)

    greet(p > 0, p - 1, d)
    greet(p < planes - 1, p + 1, d)
    greet(d > 0, p, d - 1)
    greet(d < depths - 1, p, d + 1)
    for source in range(depths):
        low_there = p - source >= 0
        if source == 0:
            low_there = low_there & (d != 0)
        greet(low_there, p - source, source)
        greet(p - source - 1 >= 0, p - source - 1, source)

    table[...] = jnp.zeros_like(table)
    table[:channels, :knots] = transfer[...]
    flat = table[:8]
    knot_index = lax.broadcasted_iota(jnp.int32, flat.shape, 1)
    slope = jnp.where(knot_index < knots - 1, pltpu.roll(flat, lanes - 1, 1) - flat, 0.0)
    table[8:16] = slope

    def one(condition):
        return jnp.where(condition, 1, 0)

    partners = one(p > 0) + one(p < planes - 1) + one(d > 0) + one(d < depths - 1)
    partners += one(p + d < planes) * (depths - one(d == 0))
    partners += one(p + d + 1 < planes) * depths
    pl.semaphore_wait(barrier, partners)

    def remote(src, dst, send_sem, recv_sem, plane, depth):
        return pltpu.make_async_remote_copy(
            src_ref=src, dst_ref=dst, send_sem=send_sem, recv_sem=recv_sem,
            device_id=(plane, depth), device_id_type=MESH,
        )

    x_up = remote(volume.at[cells_x - 1], side_x.at[0], x_send.at[0], x_recv.at[0], p + 1, d)
    x_down = remote(volume.at[0], side_x.at[1], x_send.at[1], x_recv.at[1], p - 1, d)
    z_up = remote(edge.at[1], side_z.at[0], z_send.at[0], z_recv.at[0], p, d + 1)
    z_down = remote(edge.at[0], side_z.at[1], z_send.at[1], z_recv.at[1], p, d - 1)
    has_below, has_above = p > 0, p < planes - 1
    has_front, has_back = d > 0, d < depths - 1
    pl.when(has_above)(x_up.start)
    pl.when(has_below)(x_down.start)
    for x in range(cells_x):
        loads[x].wait()

    def turn(x, carry):
        turned = vol[x].T
        tall[x + 1, PAD : PAD + cells_z] = turned
        fields[0, x] = turned.astype(jnp.bfloat16)
        edge[0, x] = turned[:1]
        edge[1, x] = turned[cells_z - 1 :]
        return carry

    lax.fori_loop(0, cells_x, turn, 0, unroll=True)

    pl.when(has_back)(z_up.start)
    pl.when(has_front)(z_down.start)

    def resampled(field, first, count):
        block = fields[field, first : first + count].reshape(count * cells_z, cells_y)
        found = lax.dot_general(
            block, mat[...], (((1,), (1,)), ((), ())), preferred_element_type=jnp.float32
        )
        samples[field, first : first + count] = found.reshape(count, cells_z, cells_y)

    loads[cells_x].wait()
    resampled(0, 0, cells_x)

    def slope_y(step, carry):
        x, part = step // cells_x, step % cells_x
        block = tall[x + 1, pl.ds(pl.multiple_of(PAD + part * group, 8), group)]
        lane = lax.broadcasted_iota(jnp.int32, block.shape, 1)
        upper = jnp.where(lane < cells_y - 1, pltpu.roll(block, cells_y - 1, 1), 0.0)
        lower = jnp.where(lane > 0, pltpu.roll(block, 1, 1), 0.0)
        fields[2, x, pl.ds(pl.multiple_of(part * group, 16), group)] = (
            (upper - lower) * 0.5
        ).astype(jnp.bfloat16)
        return carry

    lax.fori_loop(0, cells_x * cells_x, slope_y, 0, unroll=True)
    resampled(2, 0, cells_x)

    loads[cells_x + 1].wait()
    rows[:, columns:] = jnp.zeros_like(rows[:, columns:])
    nearest = jnp.minimum(p + d, planes - 1) * cells_x
    offset = nearest % 8
    around = pl.ds(pl.multiple_of(nearest - offset, 8), 16)
    for end in range(2):
        found = rows[end, around]
        aligned = jnp.where(offset == 0, found[: 2 * cells_x], found[8 - cells_x : 8 + cells_x])
        for pixel in range(2 * cells_x):
            window[end, pixel] = aligned[pixel : pixel + 1]

    scale = (knots - 1) / 5.0
    step_size = 2.0 / (depths * cells_z)

    def density(step, carry):
        x, part = step // cells_x, step % cells_x
        at = pl.ds(pl.multiple_of(part * group, 16), group)
        index = d * cells_z + part * group + lax.broadcasted_iota(jnp.int32, (group, lanes), 0)
        for tile in range(cells_y // lanes):
            here = slice(tile * lanes, (tile + 1) * lanes)
            spot = jnp.clip(samples[0, x, at, here] * scale + 2.5 * scale, 0.0, knots - 1.0)
            knot = spot.astype(jnp.int32)
            rest = spot - knot.astype(jnp.float32)

            def looked_up(channel):
                base = jnp.broadcast_to(table[channel : channel + 1], (group, lanes))
                tilt = jnp.broadcast_to(table[8 + channel : 9 + channel], (group, lanes))
                return jnp.take_along_axis(
                    base, knot, axis=1, mode="promise_in_bounds"
                ) + rest * jnp.take_along_axis(tilt, knot, axis=1, mode="promise_in_bounds")

            first = window[0, x + part, :, here]
            last = window[1, x + part, :, here]
            inside = (index >= first) & (index < last)
            taus[x, at, here] = jnp.where(inside, step_size * looked_up(3), 0.0)
            for channel in range(3):
                tint[channel, x, at, here] = looked_up(channel)
        return carry

    lax.fori_loop(0, cells_x * cells_x, density, 0, unroll=True)

    row = lax.broadcasted_iota(jnp.int32, (cells_z, cells_z), 0)
    column = lax.broadcasted_iota(jnp.int32, (cells_z, cells_z), 1)
    earlier = jnp.where((column < row) & (column // group == row // group), 1.0, 0.0)
    earlier = earlier.astype(jnp.bfloat16)
    earlier = jnp.concatenate([earlier, earlier], axis=1)
    for x in range(cells_x):
        tau = taus[x]
        high = tau.astype(jnp.bfloat16)
        low = (tau - high.astype(jnp.float32)).astype(jnp.bfloat16)
        before[x] = jnp.dot(
            earlier, jnp.concatenate([high, low], axis=0), preferred_element_type=jnp.float32
        )

    pl.when(has_front)(z_down.wait_send)
    pl.when(has_back)(z_up.wait_send)
    pl.when(has_front)(z_up.wait_recv)
    pl.when(has_back)(z_down.wait_recv)

    @pl.when(jnp.logical_not(has_front))
    def _():
        side_z[0] = jnp.zeros_like(side_z[0])

    @pl.when(jnp.logical_not(has_back))
    def _():
        side_z[1] = jnp.zeros_like(side_z[1])

    for x in range(cells_x):
        tall[x + 1, PAD - 1 : PAD] = side_z[0, x]
        tall[x + 1, PAD + cells_z : PAD + cells_z + 1] = side_z[1, x]
    for x in range(cells_x):
        ahead = tall[x + 1, PAD + 1 : PAD + 1 + cells_z]
        behind = tall[x + 1, PAD - 1 : PAD - 1 + cells_z]
        fields[3, x] = ((ahead - behind) * 0.5).astype(jnp.bfloat16)
    resampled(3, 0, cells_x)

    light_x, light_y, light_z = light[0], light[1], light[2]

    def tiles(first, count):
        for x in range(first, first + count):
            for part in range(cells_x):
                for tile in range(cells_y // lanes):
                    at = slice(part * group, (part + 1) * group)
                    yield x, part, at, slice(tile * lanes, (tile + 1) * lanes)

    def prepared(x, part, at, here):
        grad_y = samples[2, x, at, here]
        grad_z = samples[3, x, at, here]
        along = grad_y * light_y + grad_z * light_z
        norm = grad_y * grad_y + grad_z * grad_z + 1.0
        tau = taus[x, at, here]
        ahead = before[x, at, here]
        pieces[part, 3, x, :, here] = ahead[group - 1 :] + tau[group - 1 :]
        return along, norm, jnp.exp(-ahead) * (1.0 - jnp.exp(-tau))

    def finished(x, part, at, here, along, norm, weight):
        grad_x = samples[1, (x - 1) % cells_x, at, here]
        lit = 0.7 * jnp.abs(along + grad_x * light_x) * lax.rsqrt(norm + grad_x * grad_x)
        weight = weight * (lit + 0.3)
        for channel in range(3):
            pieces[part, channel, x, :, here] = jnp.sum(
                weight * tint[channel, x, at, here], axis=0, keepdims=True
            )

    def slope_x(x):
        ahead = tall[x + 2, PAD : PAD + cells_z]
        behind = tall[x, PAD : PAD + cells_z]
        fields[1, (x - 1) % cells_x] = ((ahead - behind) * 0.5).astype(jnp.bfloat16)

    for x in range(1, cells_x - 1):
        slope_x(x)
    resampled(1, 0, cells_x - 2)
    for place in tiles(1, cells_x - 2):
        finished(*place, *prepared(*place))
    for edge_x in (0, cells_x - 1):
        for place in tiles(edge_x, 1):
            x, part, at, here = place
            along, norm, weight = prepared(*place)
            samples[2, x, at, here] = along
            samples[3, x, at, here] = norm
            before[x, at, here] = weight
    pl.when(has_above)(x_up.wait_send)
    pl.when(has_below)(x_down.wait_send)
    pl.when(has_below)(x_up.wait_recv)
    pl.when(has_above)(x_down.wait_recv)

    @pl.when(jnp.logical_not(has_below))
    def _():
        side_x[0] = jnp.zeros_like(side_x[0])

    @pl.when(jnp.logical_not(has_above))
    def _():
        side_x[1] = jnp.zeros_like(side_x[1])

    tall[0, PAD : PAD + cells_z] = side_x[0].T
    tall[cells_x + 1, PAD : PAD + cells_z] = side_x[1].T
    slope_x(0)
    slope_x(cells_x - 1)
    resampled(1, cells_x - 2, 2)
    for edge_x in (0, cells_x - 1):
        for place in tiles(edge_x, 1):
            x, part, at, here = place
            finished(
                *place, samples[2, x, at, here], samples[3, x, at, here], before[x, at, here]
            )

    def placed(part, channel):
        ahead = [jnp.zeros((part, cells_y), jnp.float32)] if part else []
        block = [pieces[part, channel, x] for x in range(cells_x)]
        rest = [jnp.zeros((cells_x - part, cells_y), jnp.float32)]
        return jnp.concatenate(ahead + block + rest, axis=0)

    color, remain = None, None
    for part in range(cells_x - 1, -1, -1):
        clear = jnp.exp(-placed(part, 3))
        front = [placed(part, channel) for channel in range(3)]
        if color is None:
            color, remain = front, clear
        else:
            color = [front[channel] + clear * color[channel] for channel in range(3)]
            remain = clear * remain
    for channel, value in enumerate(color + [remain]):
        for half in range(2):
            for block in range(depths):
                send[half, block, channel] = value[
                    half * cells_x : (half + 1) * cells_x, block * share : (block + 1) * share
                ]

    sends = []
    for half in range(2):
        for block in range(depths):
            there = p + d + half < planes
            if half == 0 and block == 0:
                there = there & (d != 0)
            copy = remote(
                send.at[half, block], recv.at[d, half], p_send.at[half, block],
                p_recv.at[d, half], p + d + half, block,
            )
            pl.when(there)(copy.start)
            sends.append((there, copy))

    @pl.when(d == 0)
    def _():
        recv[0, 0] = send[0, 0]

    for source in range(depths):
        for half in range(2):
            there = p - source - half >= 0

            @pl.when(jnp.logical_not(there))
            def _():
                recv[source, half, :3] = jnp.zeros_like(recv[source, half, :3])
                recv[source, half, 3] = jnp.ones_like(recv[source, half, 3])

            if half == 0 and source == 0:
                there = there & (d != 0)
            arrival = remote(
                send.at[half, 0], recv.at[source, half], p_send.at[half, 0],
                p_recv.at[source, half], p, d,
            )
            pl.when(there)(arrival.wait_recv)

    color = [recv[0, 0, channel] for channel in range(3)]
    remain = recv[0, 0, 3]
    for source in range(depths):
        for half in range(2):
            if source == 0 and half == 0:
                continue
            color = [
                color[channel] + remain * recv[source, half, channel] for channel in range(3)
            ]
            remain = remain * recv[source, half, 3]
    for channel in range(3):
        out[channel] = color[channel]
    out[3] = 1.0 - remain
    for there, copy in sends:
        pl.when(there)(copy.wait_send)


def body(volume, resample, transfer, light, ray_bounds):
    cells_x, cells_y, cells_z = volume.shape
    planes = lax.axis_size("plane")
    depths = lax.axis_size("depth")
    share = cells_y // depths
    f32 = jnp.float32
    dma = pltpu.SemaphoreType.DMA
    return pl.pallas_call(
        functools.partial(kernel, planes, depths),
        out_shape=jax.ShapeDtypeStruct((4, cells_x, share), f32),
        in_specs=[
            pl.BlockSpec(memory_space=pltpu.HBM),
            pl.BlockSpec(memory_space=pltpu.HBM),
            pl.BlockSpec(memory_space=pltpu.HBM),
            pl.BlockSpec(memory_space=pltpu.VMEM),
            pl.BlockSpec(memory_space=pltpu.SMEM),
        ],
        out_specs=pl.BlockSpec(memory_space=pltpu.VMEM),
        scratch_shapes=[
            pltpu.VMEM((cells_x, cells_y, cells_z), f32),
            pltpu.VMEM(resample.shape, resample.dtype),
            pltpu.VMEM((2, ray_bounds.shape[1] + 8, cells_y), ray_bounds.dtype),
            pltpu.VMEM((2, 2 * cells_x, 1, cells_y), ray_bounds.dtype),
            pltpu.VMEM((2, cells_y, cells_z), f32),
            pltpu.VMEM((2, cells_x, 1, cells_y), f32),
            pltpu.VMEM((2, cells_x, 1, cells_y), f32),
            pltpu.VMEM((cells_x + 2, cells_z + 2 * PAD, cells_y), f32),
            pltpu.VMEM((4, cells_x, cells_z, cells_y), jnp.bfloat16),
            pltpu.VMEM((4, cells_x, cells_z, cells_y), f32),
            pltpu.VMEM((cells_x, cells_z, cells_y), f32),
            pltpu.VMEM((cells_x, cells_z, cells_y), f32),
            pltpu.VMEM((3, cells_x, cells_z, cells_y), f32),
            pltpu.VMEM((cells_x, 4, cells_x, 1, cells_y), f32),
            pltpu.VMEM((16, 128), f32),
            pltpu.VMEM((2, depths, 4, cells_x, share), f32),
            pltpu.VMEM((depths, 2, 4, cells_x, share), f32),
            dma((cells_x + 2,)),
            dma((2,)),
            dma((2,)),
            dma((2,)),
            dma((2,)),
            dma((2, depths)),
            dma((depths, 2)),
        ],
        compiler_params=pltpu.CompilerParams(
            collective_id=0, has_side_effects=True, vmem_limit_bytes=64 * 1024 * 1024
        ),
    )(volume, resample, ray_bounds, transfer.T, light)


def solution(mesh):
    in_specs = (P("plane", None, "depth"), P(), P(), P(), P())
    out_specs = P(None, "plane", "depth")
    return jax.shard_map(body, mesh=mesh, in_specs=in_specs, out_specs=out_specs, check_vma=False)
```

```python
import functools

import jax
import jax.numpy as jnp
from jax import lax
from jax.experimental import pallas as pl
from jax.experimental.pallas import tpu as pltpu
from jax.sharding import PartitionSpec as P

MESH = pl.DeviceIdType.MESH
PAD = 8
VMEM_BYTES = 64 * 1024 * 1024


def at_knots(row, knot):
    numbers = lax.GatherDimensionNumbers(
        offset_dims=(), collapsed_slice_dims=(1,), start_index_map=(1,),
        operand_batching_dims=(0,), start_indices_batching_dims=(0,),
    )
    return lax.gather(
        row, knot[:, :, None], numbers, slice_sizes=(1, 1),
        mode=lax.GatherScatterMode.PROMISE_IN_BOUNDS,
    )


def kernel(
    planes, depths, volume, resample, bounds, transfer, light, out,
    vol, mat, rows, window, side_x, edge, side_z, tall, fields, samples, taus, before, tint, pieces,
    table, send, recv, local_sem, x_send, x_recv, z_send, z_recv, p_send, p_recv,
):
    cells_x, cells_y, cells_z = volume.shape
    channels, knots = transfer.shape
    columns = bounds.shape[1]
    share = cells_y // depths
    group = cells_z // cells_x
    lanes = 128
    p = lax.axis_index("plane")
    d = lax.axis_index("depth")

    loads = [pltpu.make_async_copy(volume.at[x], vol.at[x], local_sem.at[x]) for x in range(cells_x)]
    loads.append(pltpu.make_async_copy(resample, mat, local_sem.at[cells_x]))
    loads.append(pltpu.make_async_copy(bounds, rows.at[:, :columns], local_sem.at[cells_x + 1]))
    for load in loads:
        load.start()

    barrier = pltpu.get_barrier_semaphore()

    def greet(condition, plane, depth):
        @pl.when(condition)
        def _():
            pl.semaphore_signal(barrier, inc=1, device_id=(plane, depth), device_id_type=MESH)

    greet(p > 0, p - 1, d)
    greet(p < planes - 1, p + 1, d)
    greet(d > 0, p, d - 1)
    greet(d < depths - 1, p, d + 1)
    for source in range(depths):
        low_there = p - source >= 0
        if source == 0:
            low_there = low_there & (d != 0)
        greet(low_there, p - source, source)
        greet(p - source - 1 >= 0, p - source - 1, source)

    table[...] = jnp.zeros_like(table)
    step_size = 2.0 / (depths * cells_z)
    table[:channels, :knots] = transfer[...]
    table[3:4, :knots] = transfer[3:4] * step_size
    flat = table[:8]
    knot_index = lax.broadcasted_iota(jnp.int32, flat.shape, 1)
    slope = jnp.where(knot_index < knots - 1, pltpu.roll(flat, lanes - 1, 1) - flat, 0.0)
    table[8:16] = slope

    def one(condition):
        return jnp.where(condition, 1, 0)

    partners = one(p > 0) + one(p < planes - 1) + one(d > 0) + one(d < depths - 1)
    partners += one(p + d < planes) * (depths - one(d == 0))
    partners += one(p + d + 1 < planes) * depths
    pl.semaphore_wait(barrier, partners)

    def remote(src, dst, send_sem, recv_sem, plane, depth):
        return pltpu.make_async_remote_copy(
            src_ref=src, dst_ref=dst, send_sem=send_sem, recv_sem=recv_sem,
            device_id=(plane, depth), device_id_type=MESH,
        )

    x_up = remote(volume.at[cells_x - 1], side_x.at[0], x_send.at[0], x_recv.at[0], p + 1, d)
    x_down = remote(volume.at[0], side_x.at[1], x_send.at[1], x_recv.at[1], p - 1, d)
    z_up = remote(edge.at[1], side_z.at[0], z_send.at[0], z_recv.at[0], p, d + 1)
    z_down = remote(edge.at[0], side_z.at[1], z_send.at[1], z_recv.at[1], p, d - 1)
    has_below, has_above = p > 0, p < planes - 1
    has_front, has_back = d > 0, d < depths - 1
    pl.when(has_above)(x_up.start)
    pl.when(has_below)(x_down.start)
    for x in range(cells_x):
        loads[x].wait()

    def turn(x, carry):
        turned = vol[x].T
        tall[x + 1, PAD : PAD + cells_z] = turned
        fields[0, x] = turned.astype(jnp.bfloat16)
        edge[0, x] = turned[:1]
        edge[1, x] = turned[cells_z - 1 :]
        return carry

    lax.fori_loop(0, cells_x, turn, 0, unroll=True)

    pl.when(has_back)(z_up.start)
    pl.when(has_front)(z_down.start)

    def resampled(field, first, count):
        block = fields[field, first : first + count].reshape(count * cells_z, cells_y)
        found = lax.dot_general(
            block, mat[...], (((1,), (1,)), ((), ())), preferred_element_type=jnp.float32
        )
        samples[field, first : first + count] = found.reshape(count, cells_z, cells_y)

    loads[cells_x].wait()
    resampled(0, 0, cells_x)

    def slope_y(step, carry):
        x, part = step // cells_x, step % cells_x
        block = tall[x + 1, pl.ds(pl.multiple_of(PAD + part * group, 8), group)]
        lane = lax.broadcasted_iota(jnp.int32, block.shape, 1)
        upper = jnp.where(lane < cells_y - 1, pltpu.roll(block, cells_y - 1, 1), 0.0)
        lower = jnp.where(lane > 0, pltpu.roll(block, 1, 1), 0.0)
        fields[2, x, pl.ds(pl.multiple_of(part * group, 16), group)] = (
            upper - lower
        ).astype(jnp.bfloat16)
        return carry

    lax.fori_loop(0, cells_x * cells_x, slope_y, 0, unroll=True)
    resampled(2, 0, cells_x)

    loads[cells_x + 1].wait()
    rows[:, columns:] = jnp.zeros_like(rows[:, columns:])
    nearest = jnp.minimum(p + d, planes - 1) * cells_x
    offset = nearest % 8
    around = pl.ds(pl.multiple_of(nearest - offset, 8), 16)
    for end in range(2):
        found = rows[end, around]
        aligned = jnp.where(offset == 0, found[: 2 * cells_x], found[8 - cells_x : 8 + cells_x])
        for pixel in range(2 * cells_x):
            window[end, pixel] = aligned[pixel : pixel + 1]

    scale = (knots - 1) / 5.0

    def density(step, carry):
        x, part = step // cells_x, step % cells_x
        at = pl.ds(pl.multiple_of(part * group, 16), group)
        index = d * cells_z + part * group + lax.broadcasted_iota(jnp.int32, (group, lanes), 0)
        for tile in range(cells_y // lanes):
            here = slice(tile * lanes, (tile + 1) * lanes)
            spot = jnp.clip(samples[0, x, at, here] * scale + 2.5 * scale, 0.0, knots - 1.0)
            knot = spot.astype(jnp.int32)
            rest = spot - knot.astype(jnp.float32)

            def looked_up(channel):
                base = jnp.broadcast_to(table[channel : channel + 1], (group, lanes))
                tilt = jnp.broadcast_to(table[8 + channel : 9 + channel], (group, lanes))
                return at_knots(base, knot) + rest * at_knots(tilt, knot)

            first = window[0, x + part, :, here]
            last = window[1, x + part, :, here]
            inside = (index >= first) & (index < last)
            taus[x, at, here] = jnp.where(inside, looked_up(3), 0.0)
            for channel in range(3):
                tint[channel, x, at, here] = looked_up(channel)
        return carry

    lax.fori_loop(0, cells_x * cells_x, density, 0, unroll=True)

    row = lax.broadcasted_iota(jnp.int32, (cells_z, cells_z), 0)
    column = lax.broadcasted_iota(jnp.int32, (cells_z, cells_z), 1)
    earlier = jnp.where((column < row) & (column // group == row // group), 1.0, 0.0)
    earlier = earlier.astype(jnp.bfloat16)
    earlier = jnp.concatenate([earlier, earlier], axis=1)
    for x in range(cells_x):
        tau = taus[x]
        high = tau.astype(jnp.bfloat16)
        low = (tau - high.astype(jnp.float32)).astype(jnp.bfloat16)
        before[x] = jnp.dot(
            earlier, jnp.concatenate([high, low], axis=0), preferred_element_type=jnp.float32
        )

    pl.when(has_front)(z_down.wait_send)
    pl.when(has_back)(z_up.wait_send)
    pl.when(has_front)(z_up.wait_recv)
    pl.when(has_back)(z_down.wait_recv)

    @pl.when(jnp.logical_not(has_front))
    def _():
        side_z[0] = jnp.zeros_like(side_z[0])

    @pl.when(jnp.logical_not(has_back))
    def _():
        side_z[1] = jnp.zeros_like(side_z[1])

    for x in range(cells_x):
        tall[x + 1, PAD - 1 : PAD] = side_z[0, x]
        tall[x + 1, PAD + cells_z : PAD + cells_z + 1] = side_z[1, x]
    for x in range(cells_x):
        ahead = tall[x + 1, PAD + 1 : PAD + 1 + cells_z]
        behind = tall[x + 1, PAD - 1 : PAD - 1 + cells_z]
        fields[3, x] = (ahead - behind).astype(jnp.bfloat16)
    resampled(3, 0, cells_x)

    light_x, light_y, light_z = light[0], light[1], light[2]

    def tiles(first, count):
        for x in range(first, first + count):
            for part in range(cells_x):
                for tile in range(cells_y // lanes):
                    at = slice(part * group, (part + 1) * group)
                    yield x, part, at, slice(tile * lanes, (tile + 1) * lanes)

    def prepared(x, part, at, here):
        grad_y = samples[2, x, at, here]
        grad_z = samples[3, x, at, here]
        along = grad_y * light_y + grad_z * light_z
        norm = grad_y * grad_y + grad_z * grad_z + 4.0
        tau = taus[x, at, here]
        ahead = before[x, at, here]
        pieces[part, 3, x, :, here] = ahead[group - 1 :] + tau[group - 1 :]
        return along, norm, jnp.exp(-ahead) * (1.0 - jnp.exp(-tau))

    def finished(x, part, at, here, along, norm, weight):
        grad_x = samples[1, (x - 1) % cells_x, at, here]
        lit = 0.7 * jnp.abs(along + grad_x * light_x) * lax.rsqrt(norm + grad_x * grad_x)
        weight = weight * (lit + 0.3)
        for channel in range(3):
            pieces[part, channel, x, :, here] = jnp.sum(
                weight * tint[channel, x, at, here], axis=0, keepdims=True
            )

    def slope_x(x):
        ahead = tall[x + 2, PAD : PAD + cells_z]
        behind = tall[x, PAD : PAD + cells_z]
        fields[1, (x - 1) % cells_x] = (ahead - behind).astype(jnp.bfloat16)

    for x in range(1, cells_x - 1):
        slope_x(x)
    resampled(1, 0, cells_x - 2)
    for place in tiles(1, cells_x - 2):
        finished(*place, *prepared(*place))
    for edge_x in (0, cells_x - 1):
        for place in tiles(edge_x, 1):
            x, part, at, here = place
            along, norm, weight = prepared(*place)
            samples[2, x, at, here] = along
            samples[3, x, at, here] = norm
            before[x, at, here] = weight
    pl.when(has_above)(x_up.wait_send)
    pl.when(has_below)(x_down.wait_send)
    pl.when(has_below)(x_up.wait_recv)
    pl.when(has_above)(x_down.wait_recv)

    @pl.when(jnp.logical_not(has_below))
    def _():
        side_x[0] = jnp.zeros_like(side_x[0])

    @pl.when(jnp.logical_not(has_above))
    def _():
        side_x[1] = jnp.zeros_like(side_x[1])

    tall[0, PAD : PAD + cells_z] = side_x[0].T
    tall[cells_x + 1, PAD : PAD + cells_z] = side_x[1].T
    slope_x(0)
    slope_x(cells_x - 1)
    resampled(1, cells_x - 2, 2)
    for edge_x in (0, cells_x - 1):
        for place in tiles(edge_x, 1):
            x, part, at, here = place
            finished(
                *place, samples[2, x, at, here], samples[3, x, at, here], before[x, at, here]
            )

    def placed(part, channel):
        ahead = [jnp.zeros((part, cells_y), jnp.float32)] if part else []
        block = [pieces[part, channel, x] for x in range(cells_x)]
        rest = [jnp.zeros((cells_x - part, cells_y), jnp.float32)]
        return jnp.concatenate(ahead + block + rest, axis=0)

    color, remain = None, None
    for part in range(cells_x - 1, -1, -1):
        clear = jnp.exp(-placed(part, 3))
        front = [placed(part, channel) for channel in range(3)]
        if color is None:
            color, remain = front, clear
        else:
            color = [front[channel] + clear * color[channel] for channel in range(3)]
            remain = clear * remain
    for channel, value in enumerate(color + [remain]):
        for half in range(2):
            for block in range(depths):
                send[half, block, channel] = value[
                    half * cells_x : (half + 1) * cells_x, block * share : (block + 1) * share
                ]

    sends = []
    for half in range(2):
        for block in range(depths):
            there = p + d + half < planes
            if half == 0 and block == 0:
                there = there & (d != 0)
            copy = remote(
                send.at[half, block], recv.at[d, half], p_send.at[half, block],
                p_recv.at[d, half], p + d + half, block,
            )
            pl.when(there)(copy.start)
            sends.append((there, copy))

    @pl.when(d == 0)
    def _():
        recv[0, 0] = send[0, 0]

    for source in range(depths):
        for half in range(2):
            there = p - source - half >= 0

            @pl.when(jnp.logical_not(there))
            def _():
                recv[source, half, :3] = jnp.zeros_like(recv[source, half, :3])
                recv[source, half, 3] = jnp.ones_like(recv[source, half, 3])

            if half == 0 and source == 0:
                there = there & (d != 0)
            arrival = remote(
                send.at[half, 0], recv.at[source, half], p_send.at[half, 0],
                p_recv.at[source, half], p, d,
            )
            pl.when(there)(arrival.wait_recv)

    color = [recv[0, 0, channel] for channel in range(3)]
    remain = recv[0, 0, 3]
    for source in range(depths):
        for half in range(2):
            if source == 0 and half == 0:
                continue
            color = [
                color[channel] + remain * recv[source, half, channel] for channel in range(3)
            ]
            remain = remain * recv[source, half, 3]
    for channel in range(3):
        out[channel] = color[channel]
    out[3] = 1.0 - remain
    for there, copy in sends:
        pl.when(there)(copy.wait_send)


def body(volume, resample, transfer, light, ray_bounds):
    cells_x, cells_y, cells_z = volume.shape
    planes = lax.axis_size("plane")
    depths = lax.axis_size("depth")
    share = cells_y // depths
    room = 4 * cells_x * share * 4
    f32 = jnp.float32
    dma = pltpu.SemaphoreType.DMA
    return pl.pallas_call(
        functools.partial(kernel, planes, depths),
        out_shape=jax.ShapeDtypeStruct((4, cells_x, share), f32),
        in_specs=[
            pl.BlockSpec(memory_space=pltpu.HBM),
            pl.BlockSpec(memory_space=pltpu.HBM),
            pl.BlockSpec(memory_space=pltpu.HBM),
            pl.BlockSpec(memory_space=pltpu.VMEM),
            pl.BlockSpec(memory_space=pltpu.SMEM),
        ],
        out_specs=pl.BlockSpec(memory_space=pltpu.VMEM),
        scratch_shapes=[
            pltpu.VMEM((cells_x, cells_y, cells_z), f32),
            pltpu.VMEM(resample.shape, resample.dtype),
            pltpu.VMEM((2, ray_bounds.shape[1] + 8, cells_y), ray_bounds.dtype),
            pltpu.VMEM((2, 2 * cells_x, 1, cells_y), ray_bounds.dtype),
            pltpu.VMEM((2, cells_y, cells_z), f32),
            pltpu.VMEM((2, cells_x, 1, cells_y), f32),
            pltpu.VMEM((2, cells_x, 1, cells_y), f32),
            pltpu.VMEM((cells_x + 2, cells_z + 2 * PAD, cells_y), f32),
            pltpu.VMEM((4, cells_x, cells_z, cells_y), jnp.bfloat16),
            pltpu.VMEM((4, cells_x, cells_z, cells_y), f32),
            pltpu.VMEM((cells_x, cells_z, cells_y), f32),
            pltpu.VMEM((cells_x, cells_z, cells_y), f32),
            pltpu.VMEM((3, cells_x, cells_z, cells_y), f32),
            pltpu.VMEM((cells_x, 4, cells_x, 1, cells_y), f32),
            pltpu.VMEM((16, 128), f32),
            pltpu.VMEM((2, depths, 4, cells_x, share), f32),
            pltpu.VMEM((depths, 2, 4, cells_x, share), f32),
            dma((cells_x + 2,)),
            dma((2,)),
            dma((2,)),
            dma((2,)),
            dma((2,)),
            dma((2, depths)),
            dma((depths, 2)),
        ],
        compiler_params=pltpu.CompilerParams(
            collective_id=0, has_side_effects=True, vmem_limit_bytes=VMEM_BYTES - room
        ),
    )(volume, resample, ray_bounds, transfer.T, light)


def solution(mesh):
    in_specs = (P("plane", None, "depth"), P(), P(), P(), P())
    out_specs = P(None, "plane", "depth")
    return jax.shard_map(body, mesh=mesh, in_specs=in_specs, out_specs=out_specs, check_vma=False)
```

```python
import functools

import jax
import jax.numpy as jnp
from jax import lax
from jax.experimental import pallas as pl
from jax.experimental.pallas import tpu as pltpu
from jax.sharding import PartitionSpec as P

MESH = pl.DeviceIdType.MESH
PAD = 8
VMEM_BYTES = 64 * 1024 * 1024


def at_knots(row, knot):
    numbers = lax.GatherDimensionNumbers(
        offset_dims=(), collapsed_slice_dims=(1,), start_index_map=(1,),
        operand_batching_dims=(0,), start_indices_batching_dims=(0,),
    )
    return lax.gather(
        row, knot[:, :, None], numbers, slice_sizes=(1, 1),
        mode=lax.GatherScatterMode.PROMISE_IN_BOUNDS,
    )


def kernel(
    planes, depths, volume, resample, bounds, transfer, light, out,
    vol, mat, rows, window, side_x, edge, side_z, tall, fields, samples, taus, before, tint, pieces,
    table, send, recv, local_sem, x_send, x_recv, z_send, z_recv, p_send, p_recv,
):
    cells_x, cells_y, cells_z = volume.shape
    channels, knots = transfer.shape
    columns = bounds.shape[1]
    share = cells_y // depths
    group = cells_z // cells_x
    lanes = 128
    p = lax.axis_index("plane")
    d = lax.axis_index("depth")

    loads = [pltpu.make_async_copy(volume.at[x], vol.at[x], local_sem.at[x]) for x in range(cells_x)]
    loads.append(pltpu.make_async_copy(resample, mat, local_sem.at[cells_x]))
    loads.append(pltpu.make_async_copy(bounds, rows.at[:, :columns], local_sem.at[cells_x + 1]))
    for load in loads:
        load.start()

    barrier = pltpu.get_barrier_semaphore()

    def greet(condition, plane, depth):
        @pl.when(condition)
        def _():
            pl.semaphore_signal(barrier, inc=1, device_id=(plane, depth), device_id_type=MESH)

    greet(p > 0, p - 1, d)
    greet(p < planes - 1, p + 1, d)
    greet(d > 0, p, d - 1)
    greet(d < depths - 1, p, d + 1)
    for source in range(depths):
        low_there = p - source >= 0
        if source == 0:
            low_there = low_there & (d != 0)
        greet(low_there, p - source, source)
        greet(p - source - 1 >= 0, p - source - 1, source)

    table[...] = jnp.zeros_like(table)
    step_size = 2.0 / (depths * cells_z)
    table[:channels, :knots] = transfer[...]
    table[3:4, :knots] = transfer[3:4] * step_size
    flat = table[:8]
    knot_index = lax.broadcasted_iota(jnp.int32, flat.shape, 1)
    slope = jnp.where(knot_index < knots - 1, pltpu.roll(flat, lanes - 1, 1) - flat, 0.0)
    table[8:16] = slope

    def one(condition):
        return jnp.where(condition, 1, 0)

    partners = one(p > 0) + one(p < planes - 1) + one(d > 0) + one(d < depths - 1)
    partners += one(p + d < planes) * (depths - one(d == 0))
    partners += one(p + d + 1 < planes) * depths
    pl.semaphore_wait(barrier, partners)

    def remote(src, dst, send_sem, recv_sem, plane, depth):
        return pltpu.make_async_remote_copy(
            src_ref=src, dst_ref=dst, send_sem=send_sem, recv_sem=recv_sem,
            device_id=(plane, depth), device_id_type=MESH,
        )

    x_up = remote(volume.at[cells_x - 1], side_x.at[0], x_send.at[0], x_recv.at[0], p + 1, d)
    x_down = remote(volume.at[0], side_x.at[1], x_send.at[1], x_recv.at[1], p - 1, d)
    z_up = remote(edge.at[1], side_z.at[0], z_send.at[0], z_recv.at[0], p, d + 1)
    z_down = remote(edge.at[0], side_z.at[1], z_send.at[1], z_recv.at[1], p, d - 1)
    has_below, has_above = p > 0, p < planes - 1
    has_front, has_back = d > 0, d < depths - 1
    pl.when(has_above)(x_up.start)
    pl.when(has_below)(x_down.start)
    for x in range(cells_x):
        loads[x].wait()

    def turn(x, carry):
        turned = vol[x].T
        tall[x + 1, PAD : PAD + cells_z] = turned
        fields[0, x] = turned.astype(jnp.bfloat16)
        edge[0, x] = turned[:1]
        edge[1, x] = turned[cells_z - 1 :]
        return carry

    lax.fori_loop(0, cells_x, turn, 0, unroll=True)

    pl.when(has_back)(z_up.start)
    pl.when(has_front)(z_down.start)

    def resampled(field, first, count):
        block = fields[field, first : first + count].reshape(count * cells_z, cells_y)
        found = lax.dot_general(
            block, mat[...], (((1,), (0,)), ((), ())), preferred_element_type=jnp.float32
        )
        samples[field, first : first + count] = found.reshape(count, cells_z, cells_y)

    loads[cells_x].wait()
    mat[...] = mat[...].T
    resampled(0, 0, cells_x)

    def slope_y(step, carry):
        x, part = step // cells_x, step % cells_x
        block = tall[x + 1, pl.ds(pl.multiple_of(PAD + part * group, 8), group)]
        lane = lax.broadcasted_iota(jnp.int32, block.shape, 1)
        upper = jnp.where(lane < cells_y - 1, pltpu.roll(block, cells_y - 1, 1), 0.0)
        lower = jnp.where(lane > 0, pltpu.roll(block, 1, 1), 0.0)
        fields[2, x, pl.ds(pl.multiple_of(part * group, 16), group)] = (
            upper - lower
        ).astype(jnp.bfloat16)
        return carry

    lax.fori_loop(0, cells_x * cells_x, slope_y, 0, unroll=True)
    resampled(2, 0, cells_x)

    loads[cells_x + 1].wait()
    rows[:, columns:] = jnp.zeros_like(rows[:, columns:])
    nearest = jnp.minimum(p + d, planes - 1) * cells_x
    offset = nearest % 8
    around = pl.ds(pl.multiple_of(nearest - offset, 8), 16)
    for end in range(2):
        found = rows[end, around]
        aligned = jnp.where(offset == 0, found[: 2 * cells_x], found[8 - cells_x : 8 + cells_x])
        for pixel in range(2 * cells_x):
            window[end, pixel] = aligned[pixel : pixel + 1]

    scale = (knots - 1) / 5.0

    def density(step, carry):
        x, part = step // cells_x, step % cells_x
        at = pl.ds(pl.multiple_of(part * group, 16), group)
        index = d * cells_z + part * group + lax.broadcasted_iota(jnp.int32, (group, lanes), 0)
        for tile in range(cells_y // lanes):
            here = slice(tile * lanes, (tile + 1) * lanes)
            spot = jnp.clip(samples[0, x, at, here] * scale + 2.5 * scale, 0.0, knots - 1.0)
            knot = spot.astype(jnp.int32)
            rest = spot - knot.astype(jnp.float32)

            def looked_up(channel):
                base = jnp.broadcast_to(table[channel : channel + 1], (group, lanes))
                tilt = jnp.broadcast_to(table[8 + channel : 9 + channel], (group, lanes))
                return at_knots(base, knot) + rest * at_knots(tilt, knot)

            first = window[0, x + part, :, here]
            last = window[1, x + part, :, here]
            inside = (index >= first) & (index < last)
            taus[x, at, here] = jnp.where(inside, looked_up(3), 0.0)
            for channel in range(3):
                tint[channel, x, at, here] = looked_up(channel)
        return carry

    lax.fori_loop(0, cells_x * cells_x, density, 0, unroll=True)

    row = lax.broadcasted_iota(jnp.int32, (cells_z, cells_z), 0)
    column = lax.broadcasted_iota(jnp.int32, (cells_z, cells_z), 1)
    earlier = jnp.where((column < row) & (column // group == row // group), 1.0, 0.0)
    earlier = earlier.astype(jnp.bfloat16)
    earlier = jnp.concatenate([earlier, earlier], axis=1)
    for x in range(cells_x):
        tau = taus[x]
        high = tau.astype(jnp.bfloat16)
        low = (tau - high.astype(jnp.float32)).astype(jnp.bfloat16)
        before[x] = jnp.dot(
            earlier, jnp.concatenate([high, low], axis=0), preferred_element_type=jnp.float32
        )

    pl.when(has_front)(z_down.wait_send)
    pl.when(has_back)(z_up.wait_send)
    pl.when(has_front)(z_up.wait_recv)
    pl.when(has_back)(z_down.wait_recv)

    @pl.when(jnp.logical_not(has_front))
    def _():
        side_z[0] = jnp.zeros_like(side_z[0])

    @pl.when(jnp.logical_not(has_back))
    def _():
        side_z[1] = jnp.zeros_like(side_z[1])

    for x in range(cells_x):
        tall[x + 1, PAD - 1 : PAD] = side_z[0, x]
        tall[x + 1, PAD + cells_z : PAD + cells_z + 1] = side_z[1, x]
    for x in range(cells_x):
        ahead = tall[x + 1, PAD + 1 : PAD + 1 + cells_z]
        behind = tall[x + 1, PAD - 1 : PAD - 1 + cells_z]
        fields[3, x] = (ahead - behind).astype(jnp.bfloat16)
    resampled(3, 0, cells_x)

    light_x, light_y, light_z = light[0], light[1], light[2]

    def tiles(first, count):
        for x in range(first, first + count):
            for part in range(cells_x):
                for tile in range(cells_y // lanes):
                    at = slice(part * group, (part + 1) * group)
                    yield x, part, at, slice(tile * lanes, (tile + 1) * lanes)

    def prepared(x, part, at, here):
        grad_y = samples[2, x, at, here]
        grad_z = samples[3, x, at, here]
        along = grad_y * light_y + grad_z * light_z
        norm = grad_y * grad_y + grad_z * grad_z + 4.0
        tau = taus[x, at, here]
        ahead = before[x, at, here]
        pieces[part, 3, x, :, here] = ahead[group - 1 :] + tau[group - 1 :]
        return along, norm, jnp.exp(-ahead) * (1.0 - jnp.exp(-tau))

    def finished(x, part, at, here, along, norm, weight):
        grad_x = samples[1, (x - 1) % cells_x, at, here]
        lit = 0.7 * jnp.abs(along + grad_x * light_x) * lax.rsqrt(norm + grad_x * grad_x)
        weight = weight * (lit + 0.3)
        for channel in range(3):
            pieces[part, channel, x, :, here] = jnp.sum(
                weight * tint[channel, x, at, here], axis=0, keepdims=True
            )

    def slope_x(x):
        ahead = tall[x + 2, PAD : PAD + cells_z]
        behind = tall[x, PAD : PAD + cells_z]
        fields[1, (x - 1) % cells_x] = (ahead - behind).astype(jnp.bfloat16)

    for x in range(1, cells_x - 1):
        slope_x(x)
    resampled(1, 0, cells_x - 2)
    for place in tiles(1, cells_x - 2):
        finished(*place, *prepared(*place))
    for edge_x in (0, cells_x - 1):
        for place in tiles(edge_x, 1):
            x, part, at, here = place
            along, norm, weight = prepared(*place)
            samples[2, x, at, here] = along
            samples[3, x, at, here] = norm
            before[x, at, here] = weight
    pl.when(has_above)(x_up.wait_send)
    pl.when(has_below)(x_down.wait_send)
    pl.when(has_below)(x_up.wait_recv)
    pl.when(has_above)(x_down.wait_recv)

    @pl.when(jnp.logical_not(has_below))
    def _():
        side_x[0] = jnp.zeros_like(side_x[0])

    @pl.when(jnp.logical_not(has_above))
    def _():
        side_x[1] = jnp.zeros_like(side_x[1])

    tall[0, PAD : PAD + cells_z] = side_x[0].T
    tall[cells_x + 1, PAD : PAD + cells_z] = side_x[1].T
    slope_x(0)
    slope_x(cells_x - 1)
    resampled(1, cells_x - 2, 2)
    for edge_x in (0, cells_x - 1):
        for place in tiles(edge_x, 1):
            x, part, at, here = place
            finished(
                *place, samples[2, x, at, here], samples[3, x, at, here], before[x, at, here]
            )

    def placed(part, channel):
        ahead = [jnp.zeros((part, cells_y), jnp.float32)] if part else []
        block = [pieces[part, channel, x] for x in range(cells_x)]
        rest = [jnp.zeros((cells_x - part, cells_y), jnp.float32)]
        return jnp.concatenate(ahead + block + rest, axis=0)

    color, remain = None, None
    for part in range(cells_x - 1, -1, -1):
        clear = jnp.exp(-placed(part, 3))
        front = [placed(part, channel) for channel in range(3)]
        if color is None:
            color, remain = front, clear
        else:
            color = [front[channel] + clear * color[channel] for channel in range(3)]
            remain = clear * remain
    for channel, value in enumerate(color + [remain]):
        for half in range(2):
            for block in range(depths):
                send[half, block, channel] = value[
                    half * cells_x : (half + 1) * cells_x, block * share : (block + 1) * share
                ]

    sends = []
    for half in range(2):
        for block in range(depths):
            there = p + d + half < planes
            if half == 0 and block == 0:
                there = there & (d != 0)
            copy = remote(
                send.at[half, block], recv.at[d, half], p_send.at[half, block],
                p_recv.at[d, half], p + d + half, block,
            )
            pl.when(there)(copy.start)
            sends.append((there, copy))

    @pl.when(d == 0)
    def _():
        recv[0, 0] = send[0, 0]

    for source in range(depths):
        for half in range(2):
            there = p - source - half >= 0

            @pl.when(jnp.logical_not(there))
            def _():
                recv[source, half, :3] = jnp.zeros_like(recv[source, half, :3])
                recv[source, half, 3] = jnp.ones_like(recv[source, half, 3])

            if half == 0 and source == 0:
                there = there & (d != 0)
            arrival = remote(
                send.at[half, 0], recv.at[source, half], p_send.at[half, 0],
                p_recv.at[source, half], p, d,
            )
            pl.when(there)(arrival.wait_recv)

    color = [recv[0, 0, channel] for channel in range(3)]
    remain = recv[0, 0, 3]
    for source in range(depths):
        for half in range(2):
            if source == 0 and half == 0:
                continue
            color = [
                color[channel] + remain * recv[source, half, channel] for channel in range(3)
            ]
            remain = remain * recv[source, half, 3]
    for channel in range(3):
        out[channel] = color[channel]
    out[3] = 1.0 - remain
    for there, copy in sends:
        pl.when(there)(copy.wait_send)


def body(volume, resample, transfer, light, ray_bounds):
    cells_x, cells_y, cells_z = volume.shape
    planes = lax.axis_size("plane")
    depths = lax.axis_size("depth")
    share = cells_y // depths
    room = 4 * cells_x * share * 4
    f32 = jnp.float32
    dma = pltpu.SemaphoreType.DMA
    return pl.pallas_call(
        functools.partial(kernel, planes, depths),
        out_shape=jax.ShapeDtypeStruct((4, cells_x, share), f32),
        in_specs=[
            pl.BlockSpec(memory_space=pltpu.HBM),
            pl.BlockSpec(memory_space=pltpu.HBM),
            pl.BlockSpec(memory_space=pltpu.HBM),
            pl.BlockSpec(memory_space=pltpu.VMEM),
            pl.BlockSpec(memory_space=pltpu.SMEM),
        ],
        out_specs=pl.BlockSpec(memory_space=pltpu.VMEM),
        scratch_shapes=[
            pltpu.VMEM((cells_x, cells_y, cells_z), f32),
            pltpu.VMEM(resample.shape, resample.dtype),
            pltpu.VMEM((2, ray_bounds.shape[1] + 8, cells_y), ray_bounds.dtype),
            pltpu.VMEM((2, 2 * cells_x, 1, cells_y), ray_bounds.dtype),
            pltpu.VMEM((2, cells_y, cells_z), f32),
            pltpu.VMEM((2, cells_x, 1, cells_y), f32),
            pltpu.VMEM((2, cells_x, 1, cells_y), f32),
            pltpu.VMEM((cells_x + 2, cells_z + 2 * PAD, cells_y), f32),
            pltpu.VMEM((4, cells_x, cells_z, cells_y), jnp.bfloat16),
            pltpu.VMEM((4, cells_x, cells_z, cells_y), f32),
            pltpu.VMEM((cells_x, cells_z, cells_y), f32),
            pltpu.VMEM((cells_x, cells_z, cells_y), f32),
            pltpu.VMEM((3, cells_x, cells_z, cells_y), f32),
            pltpu.VMEM((cells_x, 4, cells_x, 1, cells_y), f32),
            pltpu.VMEM((16, 128), f32),
            pltpu.VMEM((2, depths, 4, cells_x, share), f32),
            pltpu.VMEM((depths, 2, 4, cells_x, share), f32),
            dma((cells_x + 2,)),
            dma((2,)),
            dma((2,)),
            dma((2,)),
            dma((2,)),
            dma((2, depths)),
            dma((depths, 2)),
        ],
        compiler_params=pltpu.CompilerParams(
            collective_id=0, has_side_effects=True, vmem_limit_bytes=VMEM_BYTES - room
        ),
    )(volume, resample, ray_bounds, transfer.T, light)


def solution(mesh):
    in_specs = (P("plane", None, "depth"), P(), P(), P(), P())
    out_specs = P(None, "plane", "depth")
    return jax.shard_map(body, mesh=mesh, in_specs=in_specs, out_specs=out_specs, check_vma=False)
```
